512 devices in a mesh: row: 16 (over y_lo, x, core), col: 32 (over y_hi, z).
Axes of the slice: x: 4, y: 4 (y_hi: 2, y_lo: 2; y = y_hi * 2 + y_lo), z: 16, core: 2. Of those that a mesh axis runs over, the one named last changes fastest.
Arguments:
- p_blocks: bfloat16 [1024, 128, 256], P(('row', 'col')), may hold values from -0.5 to 0.5
- a_blocks: bfloat16 [1024, 4096, 128], P('row', 'col'), may hold values from -6 to 6
- a_owner: int32 [16, 512], P('row', 'col'), may hold values from 0 to 31
- a_row: int32 [512, 64], P('row', 'col'), may hold values from 0 to 1
- a_count: int32 [256, 64], P('row', 'col'), may hold values from 0 to 2, as said below
Outputs:
- coarse_op: bfloat16 [256, 8192, 256], P('row', 'col')
The draws below stay inside these ranges and needn't reach their ends.
Inputs may be any that keep to these rules, and one draw needn't show every extreme that they name: `a_count`: live blocks of one bucket are at most 2, and 2 is reached in every draw; the live load differs from tile to tile.
All inputs are finite; a program needn't handle non-finite values.
Results may differ from the reference program's by a relative error of at most 0.0049.
Values may be sent and summed in bfloat16 or wider, within the bound.
No kernel may reach another device: no remote copies, remote signals or barrier semaphores. Data moves between devices by JAX's collectives and lax.ppermute only.
A program may use at most 64 MiB of HBM per device.

```python
import jax
import jax.numpy as jnp
from jax import lax

B = 128
CD = 2
FD = 2
MSG = 2
NF = 1024
N_ROW = 16
N_COL = 32


def draw_a_count(key, part):
    key_level, key_base, key_spot = jax.random.split(key, 3)
    levels = jax.random.randint(key_level, (N_ROW, 1, N_COL, 1), 0, 4)
    base_draw = jax.random.randint(key_base, (N_ROW, N_ROW, N_COL, FD), 0, MSG + 1)
    counts = jnp.minimum(MSG, base_draw * levels // 2)
    flat_counts = counts.reshape(-1)
    spot_index = jax.random.randint(key_spot, (), 0, flat_counts.shape[0])
    flat_counts = flat_counts.at[spot_index].set(MSG)
    return flat_counts.reshape(N_ROW * N_ROW, N_COL * FD).astype(jnp.int32)


def set_ends(array, stream_key, low, high):
    longest = array.shape.index(max(array.shape))
    spots = []
    for shift in (0, 1):
        where = [jax.random.randint(jax.random.fold_in(stream_key, axis), (), 0, length) for axis, length in enumerate(array.shape)]
        where[longest] = (where[longest] + shift) % array.shape[longest]
        spots.append(tuple(where))
    return array.at[spots[0]].set(low).at[spots[1]].set(high)


def block_levels(own_key, shape, shards, smallest, high):
    level, own = 1.0, jax.random.fold_in(own_key, 6)
    for dim, blocks in shards:
        steps = jnp.exp(jax.random.uniform(jax.random.fold_in(own, dim), (blocks,), jnp.float32, smallest / len(shards), high / len(shards)))
        level = level * jnp.repeat(steps, shape[dim] // blocks).reshape([-1 if axis == dim else 1 for axis in range(len(shape))])
    return level


def scatter_about(key, dims, spread, reach, cuts=(), kind=jnp.bfloat16):
    factor_of = block_levels(key, dims, cuts, -0.22, 0.18) if cuts else 1.0
    entries = jax.random.normal(key, dims, jnp.float32) * spread * factor_of
    return jnp.minimum(jnp.maximum(entries, -reach), reach).astype(kind)


def setup_inputs(seed: int = 0) -> dict:
    streams_of = jax.random.split(jax.random.key(seed), 6)
    p_blocks = scatter_about(streams_of[0], (NF, B, CD * B), B ** -0.5, 0.5, ((0, 512),))
    a_blocks = scatter_about(streams_of[1], (N_ROW * N_ROW * FD * MSG, N_COL * B, B), 1.0, 6.0, ((0, 16), (1, 32)))
    a_owner = set_ends(jax.random.randint(streams_of[2], (N_ROW, N_COL * N_ROW), 0, N_COL), jax.random.fold_in(streams_of[2], 1), 0, N_COL - 1).astype(jnp.int32)
    a_row = set_ends(jax.random.randint(streams_of[3], (N_ROW * N_ROW * FD, N_COL * MSG), 0, FD), jax.random.fold_in(streams_of[3], 1), 0, FD - 1).astype(jnp.int32)
    a_count = draw_a_count(jax.random.fold_in(streams_of[5], 71), 0)
    return {"p_blocks": p_blocks, "a_blocks": a_blocks, "a_owner": a_owner, "a_row": a_row, "a_count": a_count}


def reference(p_blocks, a_blocks, a_owner, a_row, a_count):
    coarse_width = CD * B
    slot_count = N_ROW * FD * MSG
    prolong = p_blocks.reshape(N_ROW, N_COL, FD, B, coarse_width)
    blocks = a_blocks.reshape(N_ROW, slot_count, N_COL, B, B)
    owners = a_owner.reshape(N_ROW, N_COL, N_ROW)
    row_index = a_row.reshape(N_ROW, N_ROW, FD, N_COL, MSG)
    counts = a_count.reshape(N_ROW, N_ROW, N_COL, FD)

    def one_tile(tile_index):
        row_pos = tile_index // N_COL
        col_pos = tile_index % N_COL
        tile_blocks = blocks[row_pos, :, col_pos].reshape(N_ROW, FD, MSG, B, B)
        owner_cols = owners[row_pos, col_pos]
        local_rows = row_index[row_pos, :, :, col_pos]
        row_group = prolong[row_pos]
        chosen = row_group[owner_cols[:, None, None], local_rows]
        slot_terms = lax.dot_general(tile_blocks.astype(jnp.float32), chosen.astype(jnp.float32),
                                     (((3,), (3,)), ((0, 1, 2), (0, 1, 2))),
                                     precision=lax.Precision.HIGHEST)
        is_live = jnp.arange(MSG, dtype=jnp.int32)[None, None, :] < counts[row_pos, :, col_pos][:, :, None]
        slot_terms = jnp.where(is_live[..., None, None], slot_terms, 0.0).astype(jnp.bfloat16)
        slot_terms = lax.optimization_barrier(slot_terms)
        summed = jnp.sum(slot_terms.astype(jnp.float32), axis=2)
        col_group = prolong[:, col_pos]
        return lax.dot_general(summed, col_group.astype(jnp.float32),
                               (((1, 2), (1, 2)), ((0,), (0,))),
                               precision=lax.Precision.HIGHEST)

    pieces = lax.map(one_tile, jnp.arange(N_ROW * N_COL, dtype=jnp.int32))
    pieces = pieces.reshape(N_ROW, N_COL, N_ROW, coarse_width, coarse_width).transpose(2, 0, 1, 3, 4)
    return pieces.reshape(N_ROW * N_ROW, N_COL * coarse_width, coarse_width).astype(jnp.bfloat16)
```

```python
import functools

import jax
import jax.numpy as jnp
import numpy as np
from jax import lax
from jax.experimental import pallas as pl
from jax.experimental.pallas import tpu as pltpu
from jax.sharding import Mesh
from jax.sharding import PartitionSpec as P

AXES = ("yl", "x", "core", "yh", "z")
ROW, COL = AXES[:3], AXES[3:]
EARLY = 112
VMEM = 40 * 1024 * 1024


def params():
    return pltpu.CompilerParams(vmem_limit_bytes=VMEM)


def in_vmem():
    return pl.BlockSpec(memory_space=pltpu.VMEM)


def in_smem():
    return pl.BlockSpec(memory_space=pltpu.SMEM)


def split_kernel(p_ref, early_ref, late_ref):
    for j in range(p_ref.shape[0]):
        turned = p_ref[j].T
        if EARLY:
            early_ref[j] = turned[:EARLY]
        late_ref[j] = turned[EARLY:]


def split_panels(p):
    fine, block, width = p.shape
    late = width - EARLY
    return pl.pallas_call(
        split_kernel,
        out_shape=(
            jax.ShapeDtypeStruct((fine, EARLY, block), p.dtype),
            jax.ShapeDtypeStruct((fine, late, block), p.dtype),
        ),
        in_specs=[in_vmem()],
        out_specs=(in_vmem(), in_vmem()),
        compiler_params=params(),
    )(p)


def terms(owner_ref, row_ref, count_ref, panel, a_ref, out_ref):
    groups, _, width = out_ref.shape
    block = a_ref.shape[2]
    fine = width // block

    def bucket(s, carry):
        owner = owner_ref[0, s]
        for g in range(fine):
            count = count_ref[s, g]
            slots = []
            for m in range(2):
                found = panel(owner, row_ref[s * fine + g, m])
                slots.append(jnp.where(m < count, found, jnp.zeros_like(found)))
            total = jnp.dot(
                jnp.concatenate(slots, axis=1),
                a_ref[s * fine + g],
                preferred_element_type=jnp.float32,
            )
            out_ref[s, :, g * block : (g + 1) * block] = total.astype(out_ref.dtype)
        return carry

    lax.fori_loop(0, groups, bucket, 0, unroll=4)


def early_kernel(side, owner_ref, row_ref, count_ref, here_ref, own_ref, other_ref, a_ref, out_ref):
    fine = own_ref.shape[0] // side

    def panel(owner, row):
        at = (owner % side) * fine + row
        return jnp.where(owner // side == here_ref[0], own_ref[at], other_ref[at])

    terms(owner_ref, row_ref, count_ref, panel, a_ref, out_ref)


def late_kernel(side, planes, owner_ref, row_ref, count_ref, panels_ref, a_ref, out_ref):
    fine = panels_ref.shape[0] // (side * planes)

    def panel(owner, row):
        return panels_ref[((owner % side) * planes + owner // side) * fine + row]

    terms(owner_ref, row_ref, count_ref, panel, a_ref, out_ref)


def final_kernel(first, t_ref, p_ref, *rest):
    out_ref, held_ref, sems = rest[-3:]
    groups, rows, _ = t_ref.shape
    copies = []
    for r in range(groups):
        done = jnp.dot(t_ref[r], p_ref[...], preferred_element_type=jnp.float32)
        held_ref[r] = done.astype(held_ref.dtype)
        copy = pltpu.make_async_copy(
            held_ref.at[r], out_ref.at[r, pl.ds(first, rows), :], sems.at[r]
        )
        copy.start()
        copies.append(copy)
    for copy in copies:
        copy.wait()


def final(first, arrived, p, so_far=None):
    groups, rows, width = arrived.shape
    more = [] if so_far is None else [so_far]
    return pl.pallas_call(
        functools.partial(final_kernel, first),
        out_shape=jax.ShapeDtypeStruct((groups, p.shape[1], width), p.dtype),
        in_specs=[in_vmem(), in_vmem()] + [pl.BlockSpec(memory_space=pl.ANY)] * len(more),
        out_specs=pl.BlockSpec(memory_space=pl.ANY),
        scratch_shapes=[
            pltpu.VMEM((groups, rows, width), p.dtype),
            pltpu.SemaphoreType.DMA((groups,)),
        ],
        input_output_aliases={2: 0} if more else {},
        compiler_params=params(),
    )(arrived, p, *more)


def on_device(p, a, owner, row, count):
    groups = lax.axis_size(ROW)
    side = lax.axis_size("z")
    planes = lax.axis_size("yh")
    fine, block, width = p.shape
    stacked = a.reshape(groups * fine, -1, block)
    flat = p.reshape(fine * block, width)
    early, late = split_panels(p)

    def sent(kernel, rows, operands):
        specs = [in_smem()] * 3 + [in_smem() if x.ndim == 1 else in_vmem() for x in operands]
        summed = pl.pallas_call(
            kernel,
            out_shape=jax.ShapeDtypeStruct((groups, rows, fine * block), p.dtype),
            in_specs=specs + [in_vmem()],
            out_specs=in_vmem(),
            compiler_params=params(),
        )(owner, row, count, *operands, stacked)
        return lax.all_to_all(summed, ROW, split_axis=0, concat_axis=0, tiled=True)

    pair = lax.all_gather(late, "yh", axis=0, tiled=True)
    early, pair = lax.optimization_barrier((early, pair))
    late_panels = lax.all_gather(pair, "z", axis=0, tiled=True)
    own = lax.all_gather(early, "z", axis=0, tiled=True)
    other = lax.ppermute(own, "yh", [(0, 1), (1, 0)])
    here = lax.axis_index("yh").astype(jnp.int32).reshape(1)
    arrived = sent(functools.partial(early_kernel, side), EARLY, (here, own, other))
    result = final(0, arrived, flat)
    arrived = sent(functools.partial(late_kernel, side, planes), width - EARLY, (late_panels,))
    return final(EARLY, arrived, flat, result)


def solution(mesh):
    fine_mesh = Mesh(np.array(mesh.devices).reshape(2, 4, 2, 2, 16), AXES)
    in_specs = (
        P(AXES, None, None),
        P(ROW, COL, None),
        P(ROW, COL),
        P(ROW, COL),
        P(ROW, COL),
    )
    return jax.shard_map(
        on_device,
        mesh=fine_mesh,
        in_specs=in_specs,
        out_specs=P(ROW, COL, None),
        check_vma=False,
    )
```

```python
import functools

import jax
import jax.numpy as jnp
import numpy as np
from jax import lax
from jax.experimental import pallas as pl
from jax.experimental.pallas import tpu as pltpu
from jax.sharding import Mesh
from jax.sharding import PartitionSpec as P

AXES = ("yl", "x", "core", "yh", "z")
ROW, COL = AXES[:3], AXES[3:]
EARLY = 96
SOME, MOST = 24 * 1024 * 1024, 58 * 1024 * 1024
PARTS = 2


def params(limit):
    return pltpu.CompilerParams(vmem_limit_bytes=limit)


def in_vmem():
    return pl.BlockSpec(memory_space=pltpu.VMEM)


def in_smem():
    return pl.BlockSpec(memory_space=pltpu.SMEM)


def split_kernel(p_ref, early_ref, late_ref):
    for j in range(p_ref.shape[0]):
        turned = p_ref[j].T
        if EARLY:
            early_ref[j] = turned[:EARLY]
        late_ref[j] = turned[EARLY:]


def split_panels(p):
    fine, block, width = p.shape
    late = width - EARLY
    return pl.pallas_call(
        split_kernel,
        out_shape=(
            jax.ShapeDtypeStruct((fine, EARLY, block), p.dtype),
            jax.ShapeDtypeStruct((fine, late, block), p.dtype),
        ),
        in_specs=[in_vmem()],
        out_specs=(in_vmem(), in_vmem()),
        compiler_params=params(SOME),
    )(p)


def terms(fetches, panel, a_ref, a_held, out_ref, out_held, a_sems, out_sems):
    groups, _, width = out_held.shape
    block = a_held.shape[2]
    fine = width // block
    step = groups // PARTS
    reads = [
        pltpu.make_async_copy(
            a_ref.at[pl.ds(part * step * fine, step * fine)],
            a_held.at[pl.ds(part * step * fine, step * fine)],
            a_sems.at[part],
        )
        for part in range(PARTS)
    ]
    for copy in fetches + reads:
        copy.start()
    for copy in fetches:
        copy.wait()
    writes = []
    for part in range(PARTS):
        reads[part].wait()
        for s in range(part * step, (part + 1) * step):
            for g in range(fine):
                slots = [panel((s * fine + g) * 2 + m) for m in range(2)]
                total = jnp.dot(
                    jnp.concatenate(slots, axis=1),
                    a_held[s * fine + g],
                    preferred_element_type=jnp.float32,
                )
                out_held[s, :, g * block : (g + 1) * block] = total.astype(out_held.dtype)
        span = pl.ds(part * step, step)
        writes.append(pltpu.make_async_copy(out_held.at[span], out_ref.at[span], out_sems.at[part]))
        writes[-1].start()
    for copy in writes:
        copy.wait()


def early_kernel(planes, fine, table_ref, own_ref, other_ref, a_ref, out_ref, held, a_held, out_held, sems, a_sems, out_sems):
    slots = table_ref.shape[0] - 1
    here = table_ref[slots]

    def panel(slot):
        at = table_ref[slot]
        live = at >= 0
        at = jnp.maximum(at, 0)
        away = jnp.where((at // fine) % planes == here, 0, 1)
        found = held[away, at // (fine * planes) * fine + at % fine]
        return jnp.where(live, found, jnp.zeros_like(found))

    fetches = [
        pltpu.make_async_copy(ref, held.at[i], sems.at[i]) for i, ref in enumerate((own_ref, other_ref))
    ]
    terms(fetches, panel, a_ref, a_held, out_ref, out_held, a_sems, out_sems)


def late_kernel(table_ref, panels_ref, a_ref, out_ref, held, a_held, out_held, sems, a_sems, out_sems):
    def panel(slot):
        at = table_ref[slot]
        found = held[jnp.maximum(at, 0)]
        return jnp.where(at >= 0, found, jnp.zeros_like(found))

    fetches = [pltpu.make_async_copy(panels_ref, held, sems.at[0])]
    terms(fetches, panel, a_ref, a_held, out_ref, out_held, a_sems, out_sems)


def final_kernel(first, t_ref, p_ref, *rest):
    out_ref, held_ref, sems = rest[-3:]
    groups, rows, _ = t_ref.shape
    copies = []
    for r in range(groups):
        done = jnp.dot(t_ref[r], p_ref[...], preferred_element_type=jnp.float32)
        held_ref[r] = done.astype(held_ref.dtype)
        copy = pltpu.make_async_copy(
            held_ref.at[r], out_ref.at[r, pl.ds(first, rows), :], sems.at[r]
        )
        copy.start()
        copies.append(copy)
    for copy in copies:
        copy.wait()


def final(first, arrived, p, so_far=None):
    groups, rows, width = arrived.shape
    more = [] if so_far is None else [so_far]
    return pl.pallas_call(
        functools.partial(final_kernel, first),
        out_shape=jax.ShapeDtypeStruct((groups, p.shape[1], width), p.dtype),
        in_specs=[in_vmem(), in_vmem()] + [pl.BlockSpec(memory_space=pl.ANY)] * len(more),
        out_specs=pl.BlockSpec(memory_space=pl.ANY),
        scratch_shapes=[
            pltpu.VMEM((groups, rows, width), p.dtype),
            pltpu.SemaphoreType.DMA((groups,)),
        ],
        input_output_aliases={2: 0} if more else {},
        compiler_params=params(SOME),
    )(arrived, p, *more)


def on_device(p, a, owner, row, count):
    groups = lax.axis_size(ROW)
    side = lax.axis_size("z")
    planes = lax.axis_size("yh")
    fine, block, width = p.shape
    stacked = a.reshape(groups * fine, -1, block)
    flat = p.reshape(fine * block, width)
    early, late = split_panels(p)

    def sent(kernel, rows, held, panels):
        summed = pl.pallas_call(
            kernel,
            out_shape=jax.ShapeDtypeStruct((groups, rows, fine * block), p.dtype),
            in_specs=[in_smem()] + [pl.BlockSpec(memory_space=pl.ANY)] * (len(panels) + 1),
            out_specs=pl.BlockSpec(memory_space=pl.ANY),
            scratch_shapes=[
                pltpu.VMEM(held, p.dtype),
                pltpu.VMEM(stacked.shape, p.dtype),
                pltpu.VMEM((groups, rows, fine * block), p.dtype),
                pltpu.SemaphoreType.DMA((len(panels),)),
                pltpu.SemaphoreType.DMA((PARTS,)),
                pltpu.SemaphoreType.DMA((PARTS,)),
            ],
            compiler_params=params(MOST),
        )(table, *panels, stacked)
        return lax.all_to_all(summed, ROW, split_axis=0, concat_axis=0, tiled=True)

    pair = lax.all_gather(late, "yh", axis=0, tiled=True)
    early, pair = lax.optimization_barrier((early, pair))
    late_panels = lax.all_gather(pair, "z", axis=0, tiled=True)
    own = lax.all_gather(early, "z", axis=0, tiled=True)
    other = lax.ppermute(own, "yh", [(0, 1), (1, 0)])

    at = (owner % side) * planes + owner // side
    at = at.reshape(groups, 1, 1) * fine + row.reshape(groups, fine, -1)
    live = jnp.arange(at.shape[2], dtype=jnp.int32)[None, None] < count[:, :, None]
    here = lax.axis_index("yh").astype(jnp.int32).reshape(1)
    table = jnp.concatenate([jnp.where(live, at, -1).reshape(-1), here])

    arrived = sent(functools.partial(early_kernel, planes, fine), EARLY, (planes, *own.shape), (own, other))
    result = final(0, arrived, flat)
    arrived = sent(late_kernel, width - EARLY, late_panels.shape, (late_panels,))
    return final(EARLY, arrived, flat, result)


def solution(mesh):
    fine_mesh = Mesh(np.array(mesh.devices).reshape(2, 4, 2, 2, 16), AXES)
    in_specs = (
        P(AXES, None, None),
        P(ROW, COL, None),
        P(ROW, COL),
        P(ROW, COL),
        P(ROW, COL),
    )
    return jax.shard_map(
        on_device,
        mesh=fine_mesh,
        in_specs=in_specs,
        out_specs=P(ROW, COL, None),
        check_vma=False,
    )
```

```python
import functools

import jax
import jax.numpy as jnp
import numpy as np
from jax import lax
from jax.experimental import pallas as pl
from jax.experimental.pallas import tpu as pltpu
from jax.sharding import Mesh
from jax.sharding import PartitionSpec as P

AXES = ("yl", "x", "core", "yh", "z")
ROW, COL = AXES[:3], AXES[3:]
EARLY = 96
SOME, MOST = 24 * 1024 * 1024, 58 * 1024 * 1024
PARTS = 2


def params(limit):
    return pltpu.CompilerParams(vmem_limit_bytes=limit)


def in_vmem():
    return pl.BlockSpec(memory_space=pltpu.VMEM)


def split_kernel(p_ref, early_ref, late_ref):
    for j in range(p_ref.shape[0]):
        turned = p_ref[j].T
        if EARLY:
            early_ref[j] = turned[:EARLY]
        late_ref[j] = turned[EARLY:]


def split_panels(p):
    fine, block, width = p.shape
    late = width - EARLY
    return pl.pallas_call(
        split_kernel,
        out_shape=(
            jax.ShapeDtypeStruct((fine, EARLY, block), p.dtype),
            jax.ShapeDtypeStruct((fine, late, block), p.dtype),
        ),
        in_specs=[in_vmem()],
        out_specs=(in_vmem(), in_vmem()),
        compiler_params=params(SOME),
    )(p)


def terms(fetches, table_fetch, panel, a_ref, a_held, out_ref, out_held, a_sems, out_sems):
    groups, _, width = out_held.shape
    block = a_held.shape[2]
    fine = width // block
    step = groups // PARTS
    reads = [
        pltpu.make_async_copy(
            a_ref.at[pl.ds(part * step * fine, step * fine)],
            a_held.at[pl.ds(part * step * fine, step * fine)],
            a_sems.at[part],
        )
        for part in range(PARTS)
    ]
    for copy in fetches + reads + [table_fetch]:
        copy.start()
    for copy in [table_fetch] + fetches:
        copy.wait()
    writes = []
    for part in range(PARTS):
        reads[part].wait()
        for s in range(part * step, (part + 1) * step):
            for g in range(fine):
                slots = [panel((s * fine + g) * 2 + m) for m in range(2)]
                total = jnp.dot(
                    jnp.concatenate(slots, axis=1),
                    a_held[s * fine + g],
                    preferred_element_type=jnp.float32,
                )
                out_held[s, :, g * block : (g + 1) * block] = total.astype(out_held.dtype)
        span = pl.ds(part * step, step)
        writes.append(pltpu.make_async_copy(out_held.at[span], out_ref.at[span], out_sems.at[part]))
        writes[-1].start()
    for copy in writes:
        copy.wait()


def early_kernel(planes, fine, table_ref, own_ref, other_ref, a_ref, out_ref, held, a_held, out_held, table, table_sem, sems, a_sems, out_sems):
    slots = table_ref.shape[0] - 1

    def panel(slot):
        at = table[slot]
        live = at >= 0
        at = jnp.maximum(at, 0)
        away = jnp.where((at // fine) % planes == table[slots], 0, 1)
        found = held[away, at // (fine * planes) * fine + at % fine]
        return jnp.where(live, found, jnp.zeros_like(found))

    fetches = [
        pltpu.make_async_copy(ref, held.at[i], sems.at[i]) for i, ref in enumerate((own_ref, other_ref))
    ]
    table_fetch = pltpu.make_async_copy(table_ref, table, table_sem)
    terms(fetches, table_fetch, panel, a_ref, a_held, out_ref, out_held, a_sems, out_sems)


def late_kernel(table_ref, panels_ref, a_ref, out_ref, held, a_held, out_held, table, table_sem, sems, a_sems, out_sems):
    def panel(slot):
        at = table[slot]
        found = held[jnp.maximum(at, 0)]
        return jnp.where(at >= 0, found, jnp.zeros_like(found))

    fetches = [pltpu.make_async_copy(panels_ref, held, sems.at[0])]
    table_fetch = pltpu.make_async_copy(table_ref, table, table_sem)
    terms(fetches, table_fetch, panel, a_ref, a_held, out_ref, out_held, a_sems, out_sems)


def final_kernel(first, t_ref, p_ref, *rest):
    out_ref, held_ref, sems = rest[-3:]
    groups, rows, _ = t_ref.shape
    copies = []
    for r in range(groups):
        done = jnp.dot(t_ref[r], p_ref[...], preferred_element_type=jnp.float32)
        held_ref[r] = done.astype(held_ref.dtype)
        copy = pltpu.make_async_copy(
            held_ref.at[r], out_ref.at[r, pl.ds(first, rows), :], sems.at[r]
        )
        copy.start()
        copies.append(copy)
    for copy in copies:
        copy.wait()


def final(first, arrived, p, so_far=None):
    groups, rows, width = arrived.shape
    more = [] if so_far is None else [so_far]
    return pl.pallas_call(
        functools.partial(final_kernel, first),
        out_shape=jax.ShapeDtypeStruct((groups, p.shape[1], width), p.dtype),
        in_specs=[in_vmem(), in_vmem()] + [pl.BlockSpec(memory_space=pl.ANY)] * len(more),
        out_specs=pl.BlockSpec(memory_space=pl.ANY),
        scratch_shapes=[
            pltpu.VMEM((groups, rows, width), p.dtype),
            pltpu.SemaphoreType.DMA((groups,)),
        ],
        input_output_aliases={2: 0} if more else {},
        compiler_params=params(SOME),
    )(arrived, p, *more)


def on_device(p, a, owner, row, count):
    groups = lax.axis_size(ROW)
    side = lax.axis_size("z")
    planes = lax.axis_size("yh")
    fine, block, width = p.shape
    stacked = a.reshape(groups * fine, -1, block)
    flat = p.reshape(fine * block, width)
    early, late = split_panels(p)

    def sent(kernel, rows, held, panels):
        summed = pl.pallas_call(
            kernel,
            out_shape=jax.ShapeDtypeStruct((groups, rows, fine * block), p.dtype),
            in_specs=[pl.BlockSpec(memory_space=pl.ANY)] * (len(panels) + 2),
            out_specs=pl.BlockSpec(memory_space=pl.ANY),
            scratch_shapes=[
                pltpu.VMEM(held, p.dtype),
                pltpu.VMEM(stacked.shape, p.dtype),
                pltpu.VMEM((groups, rows, fine * block), p.dtype),
                pltpu.SMEM(table.shape, table.dtype),
                pltpu.SemaphoreType.DMA,
                pltpu.SemaphoreType.DMA((len(panels),)),
                pltpu.SemaphoreType.DMA((PARTS,)),
                pltpu.SemaphoreType.DMA((PARTS,)),
            ],
            compiler_params=params(MOST),
        )(table, *panels, stacked)
        return lax.all_to_all(summed, ROW, split_axis=0, concat_axis=0, tiled=True)

    pair = lax.all_gather(late, "yh", axis=0, tiled=True)
    early, pair = lax.optimization_barrier((early, pair))
    late_panels = lax.all_gather(pair, "z", axis=0, tiled=True)
    own = lax.all_gather(early, "z", axis=0, tiled=True)
    other = lax.ppermute(own, "yh", [(0, 1), (1, 0)])

    at = (owner % side) * planes + owner // side
    at = at.reshape(groups, 1, 1) * fine + row.reshape(groups, fine, -1)
    live = jnp.arange(at.shape[2], dtype=jnp.int32)[None, None] < count[:, :, None]
    here = lax.axis_index("yh").astype(jnp.int32).reshape(1)
    table = jnp.concatenate([jnp.where(live, at, -1).reshape(-1), here])

    arrived = sent(functools.partial(early_kernel, planes, fine), EARLY, (planes, *own.shape), (own, other))
    result = final(0, arrived, flat)
    arrived = sent(late_kernel, width - EARLY, late_panels.shape, (late_panels,))
    return final(EARLY, arrived, flat, result)


def solution(mesh):
    fine_mesh = Mesh(np.array(mesh.devices).reshape(2, 4, 2, 2, 16), AXES)
    in_specs = (
        P(AXES, None, None),
        P(ROW, COL, None),
        P(ROW, COL),
        P(ROW, COL),
        P(ROW, COL),
    )
    return jax.shard_map(
        on_device,
        mesh=fine_mesh,
        in_specs=in_specs,
        out_specs=P(ROW, COL, None),
        check_vma=False,
    )
```

```python
import functools

import jax
import jax.numpy as jnp
import numpy as np
from jax import lax
from jax.experimental import pallas as pl
from jax.experimental.pallas import tpu as pltpu
from jax.sharding import Mesh
from jax.sharding import PartitionSpec as P

AXES = ("yl", "x", "core", "yh", "z")
ROW, COL = AXES[:3], AXES[3:]
EARLY = 112
SOME, MOST = 24 * 1024 * 1024, 58 * 1024 * 1024
PARTS = 2


def params(limit):
    return pltpu.CompilerParams(vmem_limit_bytes=limit)


def in_vmem():
    return pl.BlockSpec(memory_space=pltpu.VMEM)


def split_kernel(p_ref, early_ref, late_ref):
    for j in range(p_ref.shape[0]):
        turned = p_ref[j].T
        if EARLY:
            early_ref[j] = turned[:EARLY]
        late_ref[j] = turned[EARLY:]


def split_panels(p):
    fine, block, width = p.shape
    late = width - EARLY
    return pl.pallas_call(
        split_kernel,
        out_shape=(
            jax.ShapeDtypeStruct((fine, EARLY, block), p.dtype),
            jax.ShapeDtypeStruct((fine, late, block), p.dtype),
        ),
        in_specs=[in_vmem()],
        out_specs=(in_vmem(), in_vmem()),
        compiler_params=params(SOME),
    )(p)


def terms(fetches, table_fetch, panel, a_ref, a_held, out_ref, out_held, a_sems, out_sems):
    groups, _, width = out_held.shape
    block = a_held.shape[2]
    fine = width // block
    step = groups // PARTS
    reads = [
        pltpu.make_async_copy(
            a_ref.at[pl.ds(part * step * fine, step * fine)],
            a_held.at[pl.ds(part * step * fine, step * fine)],
            a_sems.at[part],
        )
        for part in range(PARTS)
    ]
    for copy in fetches + reads + [table_fetch]:
        copy.start()
    for copy in [table_fetch] + fetches:
        copy.wait()
    writes = []
    for part in range(PARTS):
        reads[part].wait()
        for s in range(part * step, (part + 1) * step):
            for g in range(fine):
                slots = [panel((s * fine + g) * 2 + m) for m in range(2)]
                total = jnp.dot(
                    jnp.concatenate(slots, axis=1),
                    a_held[s * fine + g],
                    preferred_element_type=jnp.float32,
                )
                out_held[s, :, g * block : (g + 1) * block] = total.astype(out_held.dtype)
        span = pl.ds(part * step, step)
        writes.append(pltpu.make_async_copy(out_held.at[span], out_ref.at[span], out_sems.at[part]))
        writes[-1].start()
    for copy in writes:
        copy.wait()


def early_kernel(planes, fine, table_ref, own_ref, other_ref, a_ref, out_ref, held, a_held, out_held, table, table_sem, sems, a_sems, out_sems):
    slots = table_ref.shape[0] - 1

    def panel(slot):
        at = table[slot]
        live = at >= 0
        at = jnp.maximum(at, 0)
        away = jnp.where((at // fine) % planes == table[slots], 0, 1)
        found = held[away, at // (fine * planes) * fine + at % fine]
        return jnp.where(live, found, jnp.zeros_like(found))

    fetches = [
        pltpu.make_async_copy(ref, held.at[i], sems.at[i]) for i, ref in enumerate((own_ref, other_ref))
    ]
    table_fetch = pltpu.make_async_copy(table_ref, table, table_sem)
    terms(fetches, table_fetch, panel, a_ref, a_held, out_ref, out_held, a_sems, out_sems)


def late_kernel(table_ref, panels_ref, a_ref, out_ref, held, a_held, out_held, table, table_sem, sems, a_sems, out_sems):
    def panel(slot):
        at = table[slot]
        found = held[jnp.maximum(at, 0)]
        return jnp.where(at >= 0, found, jnp.zeros_like(found))

    fetches = [pltpu.make_async_copy(panels_ref, held, sems.at[0])]
    table_fetch = pltpu.make_async_copy(table_ref, table, table_sem)
    terms(fetches, table_fetch, panel, a_ref, a_held, out_ref, out_held, a_sems, out_sems)


def final_kernel(first, t_ref, p_ref, *rest):
    out_ref, held_ref, sems = rest[-3:]
    groups, rows, _ = t_ref.shape
    copies = []
    for r in range(groups):
        done = jnp.dot(t_ref[r], p_ref[...], preferred_element_type=jnp.float32)
        held_ref[r] = done.astype(held_ref.dtype)
        copy = pltpu.make_async_copy(
            held_ref.at[r], out_ref.at[r, pl.ds(first, rows), :], sems.at[r]
        )
        copy.start()
        copies.append(copy)
    for copy in copies:
        copy.wait()


def final(first, arrived, p, so_far=None):
    groups, rows, width = arrived.shape
    more = [] if so_far is None else [so_far]
    return pl.pallas_call(
        functools.partial(final_kernel, first),
        out_shape=jax.ShapeDtypeStruct((groups, p.shape[1], width), p.dtype),
        in_specs=[in_vmem(), in_vmem()] + [pl.BlockSpec(memory_space=pl.ANY)] * len(more),
        out_specs=pl.BlockSpec(memory_space=pl.ANY),
        scratch_shapes=[
            pltpu.VMEM((groups, rows, width), p.dtype),
            pltpu.SemaphoreType.DMA((groups,)),
        ],
        input_output_aliases={2: 0} if more else {},
        compiler_params=params(SOME),
    )(arrived, p, *more)


def on_device(p, a, owner, row, count):
    groups = lax.axis_size(ROW)
    side = lax.axis_size("z")
    planes = lax.axis_size("yh")
    fine, block, width = p.shape
    stacked = a.reshape(groups * fine, -1, block)
    flat = p.reshape(fine * block, width)
    early, late = split_panels(p)

    def sent(kernel, rows, held, panels):
        summed = pl.pallas_call(
            kernel,
            out_shape=jax.ShapeDtypeStruct((groups, rows, fine * block), p.dtype),
            in_specs=[pl.BlockSpec(memory_space=pl.ANY)] * (len(panels) + 2),
            out_specs=pl.BlockSpec(memory_space=pl.ANY),
            scratch_shapes=[
                pltpu.VMEM(held, p.dtype),
                pltpu.VMEM(stacked.shape, p.dtype),
                pltpu.VMEM((groups, rows, fine * block), p.dtype),
                pltpu.SMEM(table.shape, table.dtype),
                pltpu.SemaphoreType.DMA,
                pltpu.SemaphoreType.DMA((len(panels),)),
                pltpu.SemaphoreType.DMA((PARTS,)),
                pltpu.SemaphoreType.DMA((PARTS,)),
            ],
            compiler_params=params(MOST),
        )(table, *panels, stacked)
        return lax.all_to_all(summed, ROW, split_axis=0, concat_axis=0, tiled=True)

    pair = lax.all_gather(late, "yh", axis=0, tiled=True)
    early, pair = lax.optimization_barrier((early, pair))
    down = [list(range(side - 1, -1, -1))]
    late_panels = lax.all_gather(pair, "z", axis=0, tiled=True, axis_index_groups=down)
    own = lax.all_gather(early, "z", axis=0, tiled=True, axis_index_groups=down)
    other = lax.ppermute(own, "yh", [(0, 1), (1, 0)])

    at = (side - 1 - owner % side) * planes + owner // side
    at = at.reshape(groups, 1, 1) * fine + row.reshape(groups, fine, -1)
    live = jnp.arange(at.shape[2], dtype=jnp.int32)[None, None] < count[:, :, None]
    here = lax.axis_index("yh").astype(jnp.int32).reshape(1)
    table = jnp.concatenate([jnp.where(live, at, -1).reshape(-1), here])

    arrived = sent(functools.partial(early_kernel, planes, fine), EARLY, (planes, *own.shape), (own, other))
    result = final(0, arrived, flat)
    arrived = sent(late_kernel, width - EARLY, late_panels.shape, (late_panels,))
    return final(EARLY, arrived, flat, result)


def solution(mesh):
    fine_mesh = Mesh(np.array(mesh.devices).reshape(2, 4, 2, 2, 16), AXES)
    in_specs = (
        P(AXES, None, None),
        P(ROW, COL, None),
        P(ROW, COL),
        P(ROW, COL),
        P(ROW, COL),
    )
    return jax.shard_map(
        on_device,
        mesh=fine_mesh,
        in_specs=in_specs,
        out_specs=P(ROW, COL, None),
        check_vma=False,
    )
```

```python
import functools

import jax
import jax.numpy as jnp
import numpy as np
from jax import lax
from jax.experimental import pallas as pl
from jax.experimental.pallas import tpu as pltpu
from jax.sharding import Mesh
from jax.sharding import PartitionSpec as P

AXES = ("yl", "x", "core", "yh", "z")
ROW, COL = AXES[:3], AXES[3:]
EARLY = 112
SOME, MOST = 24 * 1024 * 1024, 58 * 1024 * 1024
PARTS = 2


def params(limit):
    return pltpu.CompilerParams(vmem_limit_bytes=limit)


def in_vmem():
    return pl.BlockSpec(memory_space=pltpu.VMEM)


def split_kernel(p_ref, early_ref, late_ref):
    for j in range(p_ref.shape[0]):
        turned = p_ref[j].T
        if EARLY:
            early_ref[j] = turned[:EARLY]
        late_ref[j] = turned[EARLY:]


def split_panels(p):
    fine, block, width = p.shape
    late = width - EARLY
    return pl.pallas_call(
        split_kernel,
        out_shape=(
            jax.ShapeDtypeStruct((fine, EARLY, block), p.dtype),
            jax.ShapeDtypeStruct((fine, late, block), p.dtype),
        ),
        in_specs=[in_vmem()],
        out_specs=(in_vmem(), in_vmem()),
        compiler_params=params(SOME),
    )(p)


def terms(fetches, table_fetch, panel, a_ref, a_held, out_ref, out_held, a_sems, out_sems):
    groups, _, width = out_held.shape
    block = a_held.shape[2]
    fine = width // block
    step = groups // PARTS
    reads = [
        pltpu.make_async_copy(
            a_ref.at[pl.ds(part * step * fine, step * fine)],
            a_held.at[pl.ds(part * step * fine, step * fine)],
            a_sems.at[part],
        )
        for part in range(PARTS)
    ]
    for copy in fetches + reads + [table_fetch]:
        copy.start()
    for copy in [table_fetch] + fetches:
        copy.wait()
    writes = []
    for part in range(PARTS):
        reads[part].wait()
        for s in range(part * step, (part + 1) * step):
            for g in range(fine):
                slots = [panel((s * fine + g) * 2 + m) for m in range(2)]
                total = jnp.dot(
                    jnp.concatenate(slots, axis=1),
                    a_held[s * fine + g],
                    preferred_element_type=jnp.float32,
                )
                out_held[s, :, g * block : (g + 1) * block] = total.astype(out_held.dtype)
        span = pl.ds(part * step, step)
        writes.append(pltpu.make_async_copy(out_held.at[span], out_ref.at[span], out_sems.at[part]))
        writes[-1].start()
    for copy in writes:
        copy.wait()


def early_kernel(planes, fine, table_ref, own_ref, other_ref, a_ref, out_ref, held, a_held, out_held, table, table_sem, sems, a_sems, out_sems):
    slots = table_ref.shape[0] - 1

    def panel(slot):
        at = table[slot]
        live = at >= 0
        at = jnp.maximum(at, 0)
        away = jnp.where((at // fine) % planes == table[slots], 0, 1)
        found = held[away, at // (fine * planes) * fine + at % fine]
        return jnp.where(live, found, jnp.zeros_like(found))

    fetches = [
        pltpu.make_async_copy(ref, held.at[i], sems.at[i]) for i, ref in enumerate((own_ref, other_ref))
    ]
    table_fetch = pltpu.make_async_copy(table_ref, table, table_sem)
    terms(fetches, table_fetch, panel, a_ref, a_held, out_ref, out_held, a_sems, out_sems)


def late_kernel(table_ref, panels_ref, a_ref, out_ref, held, a_held, out_held, table, table_sem, sems, a_sems, out_sems):
    def panel(slot):
        at = table[slot]
        found = held[jnp.maximum(at, 0)]
        return jnp.where(at >= 0, found, jnp.zeros_like(found))

    fetches = [pltpu.make_async_copy(panels_ref, held, sems.at[0])]
    table_fetch = pltpu.make_async_copy(table_ref, table, table_sem)
    terms(fetches, table_fetch, panel, a_ref, a_held, out_ref, out_held, a_sems, out_sems)


def final_kernel(first, t_ref, p_ref, *rest):
    out_ref, held_ref, sems = rest[-3:]
    groups, rows, _ = t_ref.shape
    copies = []
    for r in range(groups):
        done = jnp.dot(t_ref[r], p_ref[...], preferred_element_type=jnp.float32)
        held_ref[r] = done.astype(held_ref.dtype)
        copy = pltpu.make_async_copy(
            held_ref.at[r], out_ref.at[r, pl.ds(first, rows), :], sems.at[r]
        )
        copy.start()
        copies.append(copy)
    for copy in copies:
        copy.wait()


def final(first, arrived, p, so_far=None):
    groups, rows, width = arrived.shape
    more = [] if so_far is None else [so_far]
    return pl.pallas_call(
        functools.partial(final_kernel, first),
        out_shape=jax.ShapeDtypeStruct((groups, p.shape[1], width), p.dtype),
        in_specs=[in_vmem(), in_vmem()] + [pl.BlockSpec(memory_space=pl.ANY)] * len(more),
        out_specs=pl.BlockSpec(memory_space=pl.ANY),
        scratch_shapes=[
            pltpu.VMEM((groups, rows, width), p.dtype),
            pltpu.SemaphoreType.DMA((groups,)),
        ],
        input_output_aliases={2: 0} if more else {},
        compiler_params=params(SOME),
    )(arrived, p, *more)


def on_device(p, a, owner, row, count):
    groups = lax.axis_size(ROW)
    side = lax.axis_size("z")
    planes = lax.axis_size("yh")
    fine, block, width = p.shape
    stacked = a.reshape(groups * fine, -1, block)
    flat = p.reshape(fine * block, width)
    early, late = split_panels(p)

    def sent(kernel, rows, held, panels):
        summed = pl.pallas_call(
            kernel,
            out_shape=jax.ShapeDtypeStruct((groups, rows, fine * block), p.dtype),
            in_specs=[pl.BlockSpec(memory_space=pl.ANY)] * (len(panels) + 2),
            out_specs=pl.BlockSpec(memory_space=pl.ANY),
            scratch_shapes=[
                pltpu.VMEM(held, p.dtype),
                pltpu.VMEM(stacked.shape, p.dtype),
                pltpu.VMEM((groups, rows, fine * block), p.dtype),
                pltpu.SMEM(table.shape, table.dtype),
                pltpu.SemaphoreType.DMA,
                pltpu.SemaphoreType.DMA((len(panels),)),
                pltpu.SemaphoreType.DMA((PARTS,)),
                pltpu.SemaphoreType.DMA((PARTS,)),
            ],
            compiler_params=params(MOST),
        )(table, *panels, stacked)
        return lax.all_to_all(summed, ROW, split_axis=0, concat_axis=0, tiled=True)

    pair = lax.all_gather(late, "yh", axis=0, tiled=True)
    early, pair = lax.optimization_barrier((early, pair))
    start = side + side // 2 - 1
    down = [[(start - i) % side for i in range(side)]]
    late_panels = lax.all_gather(pair, "z", axis=0, tiled=True, axis_index_groups=down)
    own = lax.all_gather(early, "z", axis=0, tiled=True, axis_index_groups=down)
    other = lax.ppermute(own, "yh", [(0, 1), (1, 0)])

    at = ((start - owner % side) % side) * planes + owner // side
    at = at.reshape(groups, 1, 1) * fine + row.reshape(groups, fine, -1)
    live = jnp.arange(at.shape[2], dtype=jnp.int32)[None, None] < count[:, :, None]
    here = lax.axis_index("yh").astype(jnp.int32).reshape(1)
    table = jnp.concatenate([jnp.where(live, at, -1).reshape(-1), here])

    arrived = sent(functools.partial(early_kernel, planes, fine), EARLY, (planes, *own.shape), (own, other))
    result = final(0, arrived, flat)
    arrived = sent(late_kernel, width - EARLY, late_panels.shape, (late_panels,))
    return final(EARLY, arrived, flat, result)


def solution(mesh):
    fine_mesh = Mesh(np.array(mesh.devices).reshape(2, 4, 2, 2, 16), AXES)
    in_specs = (
        P(AXES, None, None),
        P(ROW, COL, None),
        P(ROW, COL),
        P(ROW, COL),
        P(ROW, COL),
    )
    return jax.shard_map(
        on_device,
        mesh=fine_mesh,
        in_specs=in_specs,
        out_specs=P(ROW, COL, None),
        check_vma=False,
    )
```
